1024 devices in a mesh: rep: 64 (over z, core), tp: 16 (over y, x).
Axes of the slice: x: 4, y: 4, z: 32, core: 2. Of those that a mesh axis runs over, the one named last changes fastest.
Arguments:
- hidden: bfloat16 [16384, 8192], P('rep', 'tp'), may hold values from -6 to 6
- projection: bfloat16 [8192, 2048], P('tp'), may hold values from -0.0625 to 0.0625
- block_index: int32 [64, 2], P('rep'), may hold values from 0 to 1023
- block_counts: int32 [64], P('rep'), may hold values from 0 to 2, as said below
- block_change: bfloat16 [64, 2, 128, 128], P('rep'), may hold values from -0.0625 to 0.0625
- queries: bfloat16 [16384, 8192], P(('rep', 'tp')), may hold values from -160 to 160
- cached: bfloat16 [16384, 32, 2048], P(('rep', 'tp')), may hold values from -16 to 16
- lengths: int32 [16384], P(('rep', 'tp')), may hold values from 2 to 32, as said below
Outputs:
- new_entries: bfloat16 [16384, 2048], P(('rep', 'tp'))
- attention: bfloat16 [16384, 8192], P(('rep', 'tp'))
The draws below stay inside these ranges and needn't reach their ends.
Inputs may be any that keep to these rules, and one draw needn't show every extreme that they name: `block_counts`: each learner shard uses at most 2 slots, and some shard uses 2. `lengths`: some row has 32 valid positions.
All inputs are finite; a program needn't handle non-finite values.
Results may differ from the reference program's by a relative error of at most 0.005.
Values may be sent and summed in bfloat16 or wider, within the bound.
A program may use at most 64 MiB of HBM per device.

```python
import math
import jax
import jax.numpy as jnp
from jax import lax

D = 8192
QH = 64
KVH = 8
HD = 128
BLK = 128
SLOTS = 2
CTX = 32
SHARDS = 64
COLUMNS = 16
ROWS = 256
ALLROWS = 16384
KVW = 2048
GROUP = 8
NRB = 4
NCB = 16
NBLK = 64


def draw_queries(key, part):
    key = jax.random.fold_in(key, 1)
    query_scale = jnp.exp(jax.random.uniform(jax.random.fold_in(key, 11), (ALLROWS, QH, 1), jnp.float32, math.log(0.3), math.log(3.0)))
    drawn = jnp.clip(jax.random.normal(jax.random.fold_in(key, 12), (ALLROWS, QH, HD), jnp.float32), -5.0, 5.0) * query_scale
    return drawn.reshape(ALLROWS, QH * HD).astype(jnp.bfloat16)


def draw_cached(key, part):
    key = jax.random.fold_in(key, 2)
    key_scale = jnp.exp(jax.random.uniform(jax.random.fold_in(key, 21), (ALLROWS, CTX, KVH, 1), jnp.float32, math.log(0.3), math.log(3.0)))
    key_part = jnp.clip(jax.random.normal(jax.random.fold_in(key, 22), (ALLROWS, CTX, KVH, HD), jnp.float32), -5.0, 5.0) * key_scale
    value_part = jnp.clip(jax.random.normal(jax.random.fold_in(key, 23), (ALLROWS, CTX, KVH, HD), jnp.float32), -5.0, 5.0)
    joined = jnp.concatenate([key_part.reshape(ALLROWS, CTX, KVH * HD), value_part.reshape(ALLROWS, CTX, KVH * HD)], axis=2)
    return joined.astype(jnp.bfloat16)


def draw_lengths(key, part):
    key = jax.random.fold_in(key, 3)
    row_lengths = jax.random.randint(jax.random.fold_in(key, 31), (ALLROWS,), 2, CTX + 1)
    forced = jax.random.randint(jax.random.fold_in(key, 32), (), 0, ALLROWS)
    return jnp.where(jnp.arange(ALLROWS) == forced, CTX, row_lengths).astype(jnp.int32)


def draw_block_counts(key, part):
    key = jax.random.fold_in(key, 4)
    counts = jax.random.randint(jax.random.fold_in(key, 41), (SHARDS,), 0, SLOTS + 1)
    forced = jax.random.randint(jax.random.fold_in(key, 42), (), 0, SHARDS)
    return jnp.where(jnp.arange(SHARDS) == forced, SLOTS, counts).astype(jnp.int32)


def place_ends(values, rng, smallest, top_value):
    shape = values.shape
    index_at = [jax.random.randint(jax.random.fold_in(rng, axis), (), 0, shape[axis]) for axis in range(len(shape))]
    values = values.at[tuple(index_at)].set(smallest)
    longest = shape.index(max(shape))
    index_at[longest] = (index_at[longest] + 1) % shape[longest]
    return values.at[tuple(index_at)].set(top_value)


def shard_levels(stream_key, dims, shards, least, largest):
    def one(axis_at, blocks):
        steps = jax.random.uniform(jax.random.fold_in(jax.random.fold_in(stream_key, 6), axis_at), (blocks,), jnp.float32, least / len(shards), largest / len(shards))
        return jnp.repeat(jnp.exp(steps), dims[axis_at] // blocks).reshape((-1,) + (1,) * (len(dims) - axis_at - 1))

    gain = one(*shards[0])
    for cut in shards[1:]:
        gain = gain * one(*cut)
    return gain


def normal_values(rng, shape, scale, reach, split=(), kind=jnp.bfloat16):
    result = jax.random.normal(rng, shape, jnp.float32) * scale
    if len(split) > 0:
        result = shard_levels(rng, shape, split, -0.22, 0.18) * result
    return jnp.clip(result, min=-reach, max=reach).astype(kind)


def setup_inputs(seed: int = 0) -> dict:
    arg_keys = jax.random.split(jax.random.key(seed), 9)
    hidden = normal_values(arg_keys[0], (ALLROWS, D), 1.0, 6.0, ((0, 64), (1, 16)))
    projection = normal_values(arg_keys[1], (D, KVW), D ** -0.5, 0.0625, ((0, 16),))
    block_index = place_ends(jax.random.randint(arg_keys[2], (SHARDS, SLOTS), 0, COLUMNS * NBLK), jax.random.fold_in(arg_keys[2], 1), 0, (COLUMNS * NBLK) - 1).astype(jnp.int32)
    block_counts = draw_block_counts(jax.random.fold_in(arg_keys[8], 71), 0)
    block_change = normal_values(arg_keys[4], (SHARDS, SLOTS, BLK, BLK), D ** -0.5, 0.0625, ((0, 64),))
    queries = draw_queries(jax.random.fold_in(arg_keys[8], 71), 0)
    cached = draw_cached(jax.random.fold_in(arg_keys[8], 71), 0)
    lengths = draw_lengths(jax.random.fold_in(arg_keys[8], 71), 0)
    return {"hidden": hidden, "projection": projection, "block_index": block_index, "block_counts": block_counts, "block_change": block_change, "queries": queries, "cached": cached, "lengths": lengths}


def attend(query_rows, cached_rows, length_rows, new_rows):
    row_count = query_rows.shape[0]
    score_scale = 1.0 / math.sqrt(HD)
    query_heads = query_rows.astype(jnp.float32).reshape(row_count, KVH, GROUP, HD)
    cache_keys = cached_rows[:, :, :KVH * HD].astype(jnp.float32).reshape(row_count, CTX, KVH, HD)
    cache_values = cached_rows[:, :, KVH * HD:].astype(jnp.float32).reshape(row_count, CTX, KVH, HD)
    own_keys = new_rows[:, :KVH * HD].astype(jnp.float32).reshape(row_count, KVH, HD)
    own_values = new_rows[:, KVH * HD:].astype(jnp.float32).reshape(row_count, KVH, HD)
    scores = jnp.einsum('rkgd,rpkd->rkgp', query_heads, cache_keys) * score_scale
    own_scores = jnp.einsum('rkgd,rkd->rkg', query_heads, own_keys) * score_scale
    visible = (jnp.arange(CTX, dtype=jnp.int32)[None, :] < length_rows[:, None])[:, None, None, :]
    masked = jnp.where(visible, scores, -jnp.inf)
    row_top = jnp.maximum(lax.optimization_barrier(jnp.max(masked, axis=-1)), own_scores)
    exp_terms = jnp.exp(masked - row_top[..., None])
    own_terms = jnp.exp(own_scores - row_top)
    denominator = lax.optimization_barrier(jnp.sum(exp_terms, axis=-1)) + own_terms
    weights = (exp_terms / denominator[..., None]).astype(jnp.bfloat16)
    own_weight = (own_terms / denominator).astype(jnp.bfloat16)
    mixed = jnp.einsum('rkgp,rpkd->rkgd', weights.astype(jnp.float32), cache_values)
    mixed = mixed + own_weight.astype(jnp.float32)[..., None] * own_values[:, :, None, :]
    return mixed.reshape(row_count, QH * HD).astype(jnp.bfloat16)

def reference(hidden, projection, block_index, block_counts, block_change, queries, cached, lengths):
    live_slots = jnp.arange(SLOTS, dtype=jnp.int32)[None, :] < block_counts[:, None]
    pieces = block_change.astype(jnp.float32)
    pieces = jnp.where(live_slots[:, :, None, None], pieces, jnp.zeros_like(pieces))
    block_grid = jnp.zeros((COLUMNS * NBLK, BLK, BLK), jnp.float32).at[block_index.reshape(-1)].add(pieces.reshape(-1, BLK, BLK))
    change_full = block_grid.reshape(COLUMNS, NRB, NCB, BLK, BLK).transpose(0, 1, 3, 2, 4).reshape(D, KVW)

    def replica(inputs):
        hidden_rows, query_rows, cached_rows, length_rows = inputs
        base_sum = jnp.dot(hidden_rows, projection, preferred_element_type=jnp.float32)
        patch_sum = jnp.dot(hidden_rows.astype(jnp.float32), change_full, precision=lax.Precision.HIGHEST)
        new_rows = (base_sum + patch_sum).astype(jnp.bfloat16)
        return (new_rows, attend(query_rows, cached_rows, length_rows, new_rows))
    new_entries, attention = lax.map(replica, (hidden.reshape(SHARDS, ROWS, D), queries.reshape(SHARDS, ROWS, QH * HD), cached.reshape(SHARDS, ROWS, CTX, KVW), lengths.reshape(SHARDS, ROWS)))
    return (new_entries.reshape(ALLROWS, KVW), attention.reshape(ALLROWS, QH * HD))
```

```python
import functools
import math

import jax
import jax.numpy as jnp
from jax import lax
from jax.experimental import pallas as pl
from jax.experimental.pallas import tpu as pltpu
from jax.sharding import PartitionSpec as P

QH = 64
KVH = 8
HD = 128
BLK = 128
SLOTS = 2
GROUP = 8
MESH = pl.DeviceIdType.MESH
BF = jnp.bfloat16
F32 = jnp.float32
NEG = -1e30
NT = (((1,), (1,)), ((), ()))
TN = (((0,), (0,)), ((), ()))


def iota(shape, dim):
    return lax.broadcasted_iota(jnp.int32, shape, dim)


def kernel(
    n_rep,
    n_tp,
    nx,
    zlo_n,
    chunks,
    hid_hbm,
    proj_hbm,
    idx_ref,
    cnt_ref,
    chg_hbm,
    q_hbm,
    cache_hbm,
    len_ref,
    new_ref,
    att_ref,
    hid,
    proj,
    chg,
    qs,
    cache,
    gath,
    meta,
    perm,
    hp,
    hs,
    hsm,
    d32,
    dd,
    dense,
    acc,
    sendbuf,
    recv,
    bias,
    mixed,
    mstat,
    lstat,
    local_sem,
    s1_send,
    s1_recv,
    s2_send,
    s2_recv,
    s3_send,
    s3_recv,
    hs_send,
    hs_recv,
    rs_send,
    rs_recv,
):
    rep = lax.axis_index("rep")
    tp = lax.axis_index("tp")
    core = rep % 2
    z = rep // 2
    nz = n_rep // 2
    zhi_n = nz // zlo_n
    zlo = z % zlo_n
    zhi = z // zlo_n
    ny = n_tp // nx
    y = tp // nx
    x = tp % nx
    ks = BLK // n_tp
    depth = hid.shape[1]
    rows = hid.shape[0]
    nrb = depth // BLK
    kvw = proj.shape[1]
    own_rows = rows // n_tp
    slots = n_rep * SLOTS
    share = nrb * ks
    cw = kvw // chunks
    ncb = kvw // BLK

    loads = []
    for n, (src, dst) in enumerate(
        ((chg_hbm, chg), (hid_hbm, hid), (proj_hbm, proj), (q_hbm, qs), (cache_hbm, cache))
    ):
        copy = pltpu.make_async_copy(src, dst, local_sem.at[n])
        copy.start()
        loads.append(copy)

    sign = 1 - 2 * core

    def at_z(zz, cc):
        return {"rep": ((zz + 2 * nz) % nz) * 2 + cc, "tp": tp}

    def plane(o, direction):
        oy, ox = o // nx, o % nx
        return ((y + direction * oy + ny) % ny) * nx + (x + direction * ox + nx) % nx

    strides = list(range(1, zhi_n))
    steps = [d for d in range(-(zlo_n // 2 - 1), zlo_n // 2 + 1) if d != 0]

    barrier = pltpu.get_barrier_semaphore()
    for j in strides:
        pl.semaphore_signal(barrier, inc=1, device_id=at_z(z - zlo_n * j, core), device_id_type=MESH)
    for d in steps:
        pl.semaphore_signal(barrier, inc=1, device_id=at_z(z - sign * d, core), device_id_type=MESH)
    pl.semaphore_signal(barrier, inc=1, device_id=at_z(z, 1 - core), device_id_type=MESH)
    for o in range(1, n_tp):
        pl.semaphore_signal(
            barrier, inc=1, device_id={"rep": rep, "tp": plane(o, -1)}, device_id_type=MESH
        )

    place = (core * zlo_n + zlo) * zhi_n + zhi
    lane = iota((1, 128), 1)
    row_value = jnp.zeros((1, 128), F32)
    for s in range(SLOTS):
        b = idx_ref[0, s]
        target = (b & (ncb - 1)) * (n_tp * nrb) + (b >> 4) + 1
        target = jnp.where(s < cnt_ref[0], target, 0)
        row_value = jnp.where(lane == place * SLOTS + s, target.astype(F32), row_value)
    meta[core, zlo, zhi] = row_value

    pj = iota((SLOTS * ks, SLOTS * BLK), 0)
    pk = iota((SLOTS * ks, SLOTS * BLK), 1)
    pick = jnp.where(pk == (pj // ks) * BLK + tp * ks + pj % ks, 1.0, 0.0).astype(BF)
    loads[0].wait()
    own_share = jnp.dot(pick, chg[...].reshape(SLOTS * BLK, BLK), preferred_element_type=F32)
    gath[core, zlo, zhi] = own_share.astype(BF)

    pj = iota((depth, depth), 0)
    pk = iota((depth, depth), 1)
    perm[...] = jnp.where(
        pk == ((pj % share) // ks) * BLK + (pj // share) * ks + pj % ks, 1.0, 0.0
    ).astype(BF)

    pl.semaphore_wait(barrier, len(strides) + len(steps) + 1 + n_tp - 1)

    def s1_copies(j, send):
        zz = zhi if send else (zhi - j + zhi_n) % zhi_n
        dev = at_z(z + zlo_n * j, core)
        return [
            pltpu.make_async_remote_copy(
                src_ref=ref.at[core, zlo, zz],
                dst_ref=ref.at[core, zlo, zz],
                send_sem=s1_send.at[m, j - 1],
                recv_sem=s1_recv.at[m, j - 1],
                device_id=dev,
                device_id_type=MESH,
            )
            for m, ref in enumerate((gath, meta))
        ]

    def s2_copies(i, d, send):
        zz = zlo if send else (zlo - sign * d + zlo_n) % zlo_n
        dev = at_z(z + sign * d, core)
        return [
            pltpu.make_async_remote_copy(
                src_ref=ref.at[core, zz],
                dst_ref=ref.at[core, zz],
                send_sem=s2_send.at[m, i],
                recv_sem=s2_recv.at[m, i],
                device_id=dev,
                device_id_type=MESH,
            )
            for m, ref in enumerate((gath, meta))
        ]

    def s3_copies(send):
        cc = core if send else 1 - core
        return [
            pltpu.make_async_remote_copy(
                src_ref=ref.at[cc],
                dst_ref=ref.at[cc],
                send_sem=s3_send.at[m],
                recv_sem=s3_recv.at[m],
                device_id=at_z(z, 1 - core),
                device_id_type=MESH,
            )
            for m, ref in enumerate((gath, meta))
        ]

    for j in strides:
        for copy in s1_copies(j, True):
            copy.start()

    loads[1].wait()
    hp[...] = lax.dot_general(perm[...], hid[...], NT, preferred_element_type=F32).astype(BF).reshape(hp.shape)
    hs[0] = hp[tp]
    for o in range(1, n_tp):
        dest = plane(o, 1)
        pltpu.make_async_remote_copy(
            src_ref=hp.at[dest],
            dst_ref=hs.at[o],
            send_sem=hs_send,
            recv_sem=hs_recv,
            device_id={"rep": rep, "tp": dest},
            device_id_type=MESH,
        ).start()

    for j in strides:
        for copy in s1_copies(j, False):
            copy.wait_recv()
    for i, d in enumerate(steps):
        for copy in s2_copies(i, d, True):
            copy.start()

    loads[2].wait()
    tile = 512

    @pl.loop(0, kvw // tile)
    def _(n):
        cols = pl.ds(pl.multiple_of(n * tile, tile), tile)
        acc[:, cols] = jnp.dot(hid[...], proj[:, cols], preferred_element_type=F32)

    pj = iota((depth, depth), 0)
    pk = iota((depth, depth), 1)
    po = pj // share
    pc = ((y - po // nx + ny) % ny) * nx + (x - po % nx + nx) % nx
    perm[...] = jnp.where(
        pk == (pj % ks) * (n_tp * nrb) + pc * nrb + (pj % share) // ks, 1.0, 0.0
    ).astype(BF)

    def hs_wait():
        return pltpu.make_async_remote_copy(
            src_ref=hs.at[pl.ds(1, n_tp - 1)],
            dst_ref=hs.at[pl.ds(1, n_tp - 1)],
            send_sem=hs_send,
            recv_sem=hs_recv,
            device_id={"rep": rep, "tp": plane(1, 1)},
            device_id_type=MESH,
        )

    for i, d in enumerate(steps):
        for copy in s2_copies(i, d, False):
            copy.wait_recv()
    for copy in s3_copies(True):
        copy.start()

    hs_wait().wait_recv()
    hsm[...] = lax.dot_general(
        hs[...].reshape(depth, rows), perm[...], TN, preferred_element_type=F32
    ).astype(BF)

    for copy in s3_copies(False):
        copy.wait_recv()

    target_row = jnp.sum(meta[...].reshape(n_rep, 128), axis=0, keepdims=True)[:, :slots]
    d32[...] = gath[...].reshape(slots * ks, BLK).astype(F32)
    for k in range(ks):
        dd[:, k * BLK : (k + 1) * BLK] = d32[pl.ds(k, slots, stride=ks), :].astype(BF)

    per = cw // BLK
    grp = n_tp * nrb

    @pl.loop(0, chunks)
    def _(n):
        first = n * (per * grp) + 1
        ids = (iota((per * grp, slots), 0) + first).astype(F32)
        onehot = jnp.where(ids == target_row, 1.0, 0.0).astype(BF)
        for k in range(ks):
            placed = jnp.dot(
                onehot, dd[:, k * BLK : (k + 1) * BLK], preferred_element_type=F32
            ).astype(BF)
            for c in range(per):
                dense[k * grp : (k + 1) * grp, c * BLK : (c + 1) * BLK] = placed[
                    c * grp : (c + 1) * grp
                ]
        cols = pl.ds(pl.multiple_of(n * cw, cw), cw)
        total = acc[:, cols] + jnp.dot(hsm[...], dense[...], preferred_element_type=F32)
        acc[:, cols] = total
        sendbuf[n] = total.astype(BF).reshape(n_tp, own_rows, cw)
        for o in range(1, n_tp):
            dest = plane(o, 1)
            pltpu.make_async_remote_copy(
                src_ref=sendbuf.at[n, dest],
                dst_ref=recv.at[n, o - 1],
                send_sem=rs_send.at[n],
                recv_sem=rs_recv.at[n],
                device_id={"rep": rep, "tp": dest},
                device_id_type=MESH,
            ).start()

    def rs_wait(n):
        return pltpu.make_async_remote_copy(
            src_ref=recv.at[n],
            dst_ref=recv.at[n],
            send_sem=rs_send.at[n],
            recv_sem=rs_recv.at[n],
            device_id={"rep": rep, "tp": plane(1, 1)},
            device_id_type=MESH,
        )

    scale = 1.0 / math.sqrt(HD)
    loads[3].wait()
    loads[4].wait()
    span = cache.shape[1]
    positions = own_rows * span
    pos_lane = iota((1, positions), 1)
    valid_len = jnp.zeros((1, positions), jnp.int32)
    for i in range(own_rows):
        valid_len = jnp.where(pos_lane // span == i, len_ref[i], valid_len)
    seen = jnp.where(pos_lane % span < valid_len, 0.0, NEG)
    same = iota((GROUP * own_rows, positions), 0) % own_rows == iota(
        (GROUP * own_rows, positions), 1
    ) // span
    bias[...] = jnp.where(same, seen, NEG)

    def head_queries(k):
        heads = qs[:, pl.ds(pl.multiple_of(k * GROUP * HD, GROUP * HD), GROUP * HD)]
        return jnp.concatenate([heads[:, g * HD : (g + 1) * HD] for g in range(GROUP)], axis=0)

    @pl.loop(0, KVH)
    def _(k):
        keys = cache[:, :, pl.ds(pl.multiple_of(k * HD, HD), HD)].reshape(positions, HD)
        values = cache[:, :, pl.ds(pl.multiple_of((KVH + k) * HD, HD), HD)].reshape(positions, HD)
        score = lax.dot_general(head_queries(k), keys, NT, preferred_element_type=F32)
        score = score * scale + bias[...]
        top = jnp.max(score, axis=1, keepdims=True)
        e = jnp.exp(score - top)
        hi = e.astype(BF)
        lo = (e - hi.astype(F32)).astype(BF)
        mixed[k] = jnp.dot(hi, values, preferred_element_type=F32) + jnp.dot(
            lo, values, preferred_element_type=F32
        )
        mstat[k] = jnp.broadcast_to(top, (GROUP * own_rows, HD))
        lstat[k] = jnp.broadcast_to(jnp.sum(e, axis=1, keepdims=True), (GROUP * own_rows, HD))

    mine = pl.ds(pl.multiple_of(tp * own_rows, own_rows), own_rows)
    for n in range(chunks):
        rs_wait(n).wait_recv()
        cols = slice(n * cw, (n + 1) * cw)
        total = acc[mine, cols]
        for o in range(n_tp - 1):
            total = total + recv[n, o].astype(F32)
        new_ref[:, cols] = total.astype(BF)

    @pl.loop(0, KVH)
    def _(k):
        own_key = new_ref[:, pl.ds(pl.multiple_of(k * HD, HD), HD)].astype(F32)
        own_value = new_ref[:, pl.ds(pl.multiple_of((KVH + k) * HD, HD), HD)].astype(F32)
        q = head_queries(k).astype(F32)
        own = jnp.sum(
            q * jnp.concatenate([own_key] * GROUP, axis=0), axis=1, keepdims=True
        ) * scale
        top = mstat[k]
        new_top = jnp.maximum(top, own)
        a = jnp.exp(top - new_top)
        b = jnp.exp(own - new_top)
        inv = 1.0 / (lstat[k] * a + b)
        out = mixed[k] * (a * inv) + (b * inv) * jnp.concatenate([own_value] * GROUP, axis=0)
        out = out.astype(BF)
        for g in range(GROUP):
            at = pl.multiple_of(k * GROUP * HD, GROUP * HD) + g * HD
            att_ref[:, pl.ds(pl.multiple_of(at, HD), HD)] = out[g * own_rows : (g + 1) * own_rows]

    for j in strides:
        for copy in s1_copies(j, True):
            copy.wait_send()
    for i, d in enumerate(steps):
        for copy in s2_copies(i, d, True):
            copy.wait_send()
    for copy in s3_copies(True):
        copy.wait_send()
    hs_wait().wait_send()
    for n in range(chunks):
        rs_wait(n).wait_send()


def solution(mesh):
    n_rep, n_tp = mesh.shape["rep"], mesh.shape["tp"]
    nx = 4 if n_tp == 16 else 2
    nz = n_rep // 2
    zlo_n = 8 if nz == 32 else 2
    zhi_n = nz // zlo_n
    chunks = 2

    def body(hidden, projection, block_index, block_counts, block_change, queries, cached, lengths):
        rows, depth = hidden.shape
        kvw = projection.shape[1]
        own_rows, span = cached.shape[0], cached.shape[1]
        ks = BLK // n_tp
        slots = n_rep * SLOTS
        share = depth // n_tp
        cw = kvw // chunks
        heads = GROUP * own_rows
        n1, n2 = zhi_n - 1, zlo_n - 1
        any_spec = pl.BlockSpec(memory_space=pl.ANY)
        smem = pl.BlockSpec(memory_space=pltpu.SMEM)
        vmem = pl.BlockSpec(memory_space=pltpu.VMEM)
        dma = pltpu.SemaphoreType.DMA
        return pl.pallas_call(
            functools.partial(kernel, n_rep, n_tp, nx, zlo_n, chunks),
            out_shape=(
                jax.ShapeDtypeStruct((own_rows, kvw), BF),
                jax.ShapeDtypeStruct((own_rows, queries.shape[1]), BF),
            ),
            in_specs=[any_spec, any_spec, smem, smem, any_spec, any_spec, any_spec, smem],
            out_specs=(vmem, vmem),
            scratch_shapes=[
                pltpu.VMEM((rows, depth), BF),
                pltpu.VMEM((depth, kvw), BF),
                pltpu.VMEM(block_change.shape, BF),
                pltpu.VMEM(queries.shape, BF),
                pltpu.VMEM(cached.shape, BF),
                pltpu.VMEM((2, zlo_n, zhi_n, SLOTS * ks, BLK), BF),
                pltpu.VMEM((2, zlo_n, zhi_n, 1, 128), F32),
                pltpu.VMEM((depth, depth), BF),
                pltpu.VMEM((n_tp, share, rows), BF),
                pltpu.VMEM((n_tp, share, rows), BF),
                pltpu.VMEM((rows, depth), BF),
                pltpu.VMEM((slots * ks, BLK), F32),
                pltpu.VMEM((slots, ks * BLK), BF),
                pltpu.VMEM((depth, cw), BF),
                pltpu.VMEM((rows, kvw), F32),
                pltpu.VMEM((chunks, n_tp, own_rows, cw), BF),
                pltpu.VMEM((chunks, n_tp - 1, own_rows, cw), BF),
                pltpu.VMEM((heads, own_rows * span), F32),
                pltpu.VMEM((KVH, heads, HD), F32),
                pltpu.VMEM((KVH, heads, HD), F32),
                pltpu.VMEM((KVH, heads, HD), F32),
                dma((5,)),
                dma((2, n1)),
                dma((2, n1)),
                dma((2, n2)),
                dma((2, n2)),
                dma((2,)),
                dma((2,)),
                dma,
                dma,
                dma((chunks,)),
                dma((chunks,)),
            ],
            compiler_params=pltpu.CompilerParams(
                collective_id=0, has_side_effects=True, vmem_limit_bytes=48 * 1024 * 1024
            ),
        )(hidden, projection, block_index, block_counts, block_change, queries, cached, lengths)

    return jax.shard_map(
        body,
        mesh=mesh,
        in_specs=(
            P("rep", "tp"),
            P("tp", None),
            P("rep", None),
            P("rep"),
            P("rep", None, None, None),
            P(("rep", "tp"), None),
            P(("rep", "tp"), None, None),
            P(("rep", "tp")),
        ),
        out_specs=(P(("rep", "tp"), None), P(("rep", "tp"), None)),
        check_vma=False,
    )
```

```python
import functools
import math

import jax
import jax.numpy as jnp
from jax import lax
from jax.experimental import pallas as pl
from jax.experimental.pallas import tpu as pltpu
from jax.sharding import PartitionSpec as P

QH = 64
KVH = 8
HD = 128
BLK = 128
SLOTS = 2
GROUP = 8
MESH = pl.DeviceIdType.MESH
BF = jnp.bfloat16
F32 = jnp.float32
NEG = -1e30
NT = (((1,), (1,)), ((), ()))
TN = (((0,), (0,)), ((), ()))


def iota(shape, dim):
    return lax.broadcasted_iota(jnp.int32, shape, dim)


def kernel(
    n_rep,
    n_tp,
    nx,
    zlo_n,
    hid_hbm,
    proj_hbm,
    idx_ref,
    cnt_ref,
    chg_hbm,
    q_hbm,
    cache_hbm,
    len_ref,
    new_ref,
    att_ref,
    hid,
    proj,
    chg,
    qs,
    cache,
    gath,
    aim,
    perm,
    hp,
    hs,
    hsm,
    d32,
    dd,
    dense,
    acc,
    send1,
    recv1,
    mid,
    send2,
    recv2,
    bias,
    mixed,
    mstat,
    lstat,
    local_sem,
    s1_send,
    s1_recv,
    s2_send,
    s2_recv,
    s3_send,
    s3_recv,
    hs_send,
    hs_recv,
    p1_send,
    p1_recv,
    p2_send,
    p2_recv,
):
    rep = lax.axis_index("rep")
    tp = lax.axis_index("tp")
    core = rep % 2
    z = rep // 2
    nz = n_rep // 2
    zhi_n = nz // zlo_n
    zlo = z % zlo_n
    zhi = z // zlo_n
    ny = n_tp // nx
    y = tp // nx
    x = tp % nx
    ks = BLK // n_tp
    depth = hid.shape[1]
    rows = hid.shape[0]
    nrb = depth // BLK
    kvw = proj.shape[1]
    own_rows = rows // n_tp
    slots = n_rep * SLOTS
    share = nrb * ks
    cw = kvw // 2
    ncb = kvw // BLK
    tile_rows = SLOTS * ks

    loads = []
    for n, (src, dst) in enumerate(
        ((chg_hbm, chg), (hid_hbm, hid), (proj_hbm, proj), (q_hbm, qs), (cache_hbm, cache))
    ):
        copy = pltpu.make_async_copy(src, dst, local_sem.at[n])
        copy.start()
        loads.append(copy)

    sign = 1 - 2 * core

    def at_z(zz, cc):
        return {"rep": ((zz + 2 * nz) % nz) * 2 + cc, "tp": tp}

    def at_plane(o, direction):
        oy, ox = o // nx, o % nx
        return ((y + direction * oy + ny) % ny) * nx + (x + direction * ox + nx) % nx

    strides = list(range(1, zhi_n))
    steps = [d for d in range(-(zlo_n // 2 - 1), zlo_n // 2 + 1) if d != 0]

    barrier = pltpu.get_barrier_semaphore()
    for j in strides:
        pl.semaphore_signal(barrier, inc=1, device_id=at_z(z + zlo_n * j, core), device_id_type=MESH)
    for d in steps:
        pl.semaphore_signal(barrier, inc=1, device_id=at_z(z - sign * d, core), device_id_type=MESH)
    pl.semaphore_signal(barrier, inc=1, device_id=at_z(z, 1 - core), device_id_type=MESH)
    for o in range(1, n_tp):
        pl.semaphore_signal(
            barrier, inc=1, device_id={"rep": rep, "tp": at_plane(o, -1)}, device_id_type=MESH
        )

    place = (core * zlo_n + zlo) * zhi_n + zhi
    lane = iota((1, 128), 1)
    row_value = jnp.zeros((1, 128), F32)
    for s in range(SLOTS):
        b = idx_ref[0, s]
        target = (b & (ncb - 1)) * (n_tp * nrb) + (b >> 4) + 1
        target = jnp.where(s < cnt_ref[0], target, 0)
        row_value = jnp.where(lane == place * SLOTS + s, target.astype(F32), row_value)
    aim[zhi] = row_value

    pj = iota((tile_rows, 1), 0)
    pk = iota((1, SLOTS * BLK), 1)
    pick = jnp.where(pk == (pj // ks) * BLK + tp * ks + pj % ks, 1.0, 0.0).astype(BF)
    loads[0].wait()
    own_share = jnp.dot(pick, chg[...].reshape(SLOTS * BLK, BLK), preferred_element_type=F32)
    gath[core, zlo, zhi] = own_share.astype(BF)

    scale = 1.0 / math.sqrt(HD)

    def head_queries(k):
        heads = qs[:, pl.ds(pl.multiple_of(k * GROUP * HD, GROUP * HD), GROUP * HD)]
        return jnp.concatenate([heads[:, g * HD : (g + 1) * HD] for g in range(GROUP)], axis=0)

    def hs_wait():
        return pltpu.make_async_remote_copy(
            src_ref=hs.at[pl.ds(1, n_tp - 1)],
            dst_ref=hs.at[pl.ds(1, n_tp - 1)],
            send_sem=hs_send,
            recv_sem=hs_recv,
            device_id={"rep": rep, "tp": at_plane(1, 1)},
            device_id_type=MESH,
        )

    def project():
        loads[2].wait()
        tile = 512

        @pl.loop(0, kvw // tile)
        def _(n):
            cols = pl.ds(pl.multiple_of(n * tile, tile), tile)
            acc[:, cols] = jnp.dot(hid[...], proj[:, cols], preferred_element_type=F32)

    def attend_cached():
        loads[3].wait()
        loads[4].wait()
        span = cache.shape[1]
        positions = own_rows * span
        pos_lane = iota((1, positions), 1)
        valid_len = jnp.zeros((1, positions), jnp.int32)
        for i in range(own_rows):
            valid_len = jnp.where(pos_lane // span == i, len_ref[i], valid_len)
        seen = jnp.where(pos_lane % span < valid_len, 0.0, NEG)
        same = (
            iota((GROUP * own_rows, positions), 0) % own_rows
            == iota((GROUP * own_rows, positions), 1) // span
        )
        bias[...] = jnp.where(same, seen, NEG)

        @pl.loop(0, KVH)
        def _(k):
            keys = cache[:, :, pl.ds(pl.multiple_of(k * HD, HD), HD)].reshape(positions, HD)
            values = cache[:, :, pl.ds(pl.multiple_of((KVH + k) * HD, HD), HD)].reshape(positions, HD)
            score = lax.dot_general(head_queries(k), keys, NT, preferred_element_type=F32)
            score = score * scale + bias[...]
            top = jnp.max(score, axis=1, keepdims=True)
            e = jnp.exp(score - top)
            hi = e.astype(BF)
            lo = (e - hi.astype(F32)).astype(BF)
            mixed[k] = jnp.dot(hi, values, preferred_element_type=F32) + jnp.dot(
                lo, values, preferred_element_type=F32
            )
            mstat[k] = jnp.broadcast_to(top, (GROUP * own_rows, HD))
            lstat[k] = jnp.broadcast_to(jnp.sum(e, axis=1, keepdims=True), (GROUP * own_rows, HD))

    early = z < nz // 2

    loads[1].wait()

    @pl.when(early)
    def _():
        project()
        attend_cached()

    pl.semaphore_wait(barrier, len(strides) + len(steps) + 1 + n_tp - 1)

    def far_copies(j, send):
        zz = zhi if send else (zhi - j + zhi_n) % zhi_n
        return [
            pltpu.make_async_remote_copy(
                src_ref=ref,
                dst_ref=ref,
                send_sem=s1_send.at[m, j - 1],
                recv_sem=s1_recv.at[m, j - 1],
                device_id=at_z(z + zlo_n * j, core),
                device_id_type=MESH,
            )
            for m, ref in enumerate((gath.at[core, zlo, zz], aim.at[zz]))
        ]

    def near_copy(i, d, send):
        zz = zlo if send else (zlo - sign * d + zlo_n) % zlo_n
        return pltpu.make_async_remote_copy(
            src_ref=gath.at[core, zz],
            dst_ref=gath.at[core, zz],
            send_sem=s2_send.at[i],
            recv_sem=s2_recv.at[i],
            device_id=at_z(z + sign * d, core),
            device_id_type=MESH,
        )

    def core_copy(send):
        cc = core if send else 1 - core
        return pltpu.make_async_remote_copy(
            src_ref=gath.at[cc],
            dst_ref=gath.at[cc],
            send_sem=s3_send,
            recv_sem=s3_recv,
            device_id=at_z(z, 1 - core),
            device_id_type=MESH,
        )

    for j in strides:
        for copy in far_copies(j, True):
            copy.start()

    pj = iota((depth, 1), 0)
    pk = iota((1, depth), 1)
    p1 = ((pj & (share - 1)) // ks) * BLK + (pj // share) * ks + (pj & (ks - 1))
    perm[...] = jnp.where(p1 == pk, 1.0, 0.0).astype(BF)
    hp[...] = (
        lax.dot_general(perm[...], hid[...], NT, preferred_element_type=F32)
        .astype(BF)
        .reshape(hp.shape)
    )
    hs[0] = hp[tp]
    for o in range(1, n_tp):
        dest = at_plane(o, 1)
        pltpu.make_async_remote_copy(
            src_ref=hp.at[dest],
            dst_ref=hs.at[o],
            send_sem=hs_send,
            recv_sem=hs_recv,
            device_id={"rep": rep, "tp": dest},
            device_id_type=MESH,
        ).start()

    for j in strides:
        for copy in far_copies(j, False):
            copy.wait_recv()
    aims = jnp.sum(aim[...].reshape(zhi_n, 128), axis=0, keepdims=True)
    upper = jnp.floor(aims * (1.0 / 32.0))
    line = iota((tile_rows, 128), 0)
    gath[core, zlo, zhi_n] = jnp.where(
        line == 0, upper, jnp.where(line == 1, aims - 32.0 * upper, 0.0)
    ).astype(BF)
    for i, d in enumerate(steps):
        near_copy(i, d, True).start()

    @pl.when(jnp.logical_not(early))
    def _():
        project()

    pj = iota((depth, 1), 0)
    pk = iota((1, depth), 1)
    po = pj // share
    pc = ((y - po // nx + ny) & (ny - 1)) * nx + ((x - (po & (nx - 1)) + nx) & (nx - 1))
    p2 = (pj & (ks - 1)) * (n_tp * nrb) + pc * nrb + (pj & (share - 1)) // ks
    perm[...] = jnp.where(p2 == pk, 1.0, 0.0).astype(BF)

    for i, d in enumerate(steps):
        near_copy(i, d, False).wait_recv()
    core_copy(True).start()
    hs_wait().wait_recv()
    hsm[...] = lax.dot_general(
        hs[...].reshape(depth, rows), perm[...], TN, preferred_element_type=F32
    ).astype(BF)

    core_copy(False).wait_recv()

    code = jnp.sum(gath[:, :, zhi_n].reshape(2 * zlo_n, tile_rows, 128).astype(F32), axis=0)
    target_row = (code[0:1] * 32.0 + code[1:2])[:, :slots]
    d32[...] = gath[:, :, :zhi_n].reshape(slots * ks, BLK).astype(F32)
    for k in range(ks):
        dd[:, k * BLK : (k + 1) * BLK] = d32[pl.ds(k, slots, stride=ks), :].astype(BF)

    per = cw // BLK
    grp = n_tp * nrb

    def one_axis(h, phase, o):
        along_x = (h + phase) % 2 == 0
        size = nx if along_x else ny
        at = (((x if along_x else y) + o) % size).astype(jnp.int32)
        return size, at, (y * nx + at if along_x else at * nx + x)

    def first_copies(h):
        size = one_axis(h, 0, 0)[0]
        made = []
        for o in range(1, size):
            _, at, dest = one_axis(h, 0, o)
            made.append(
                pltpu.make_async_remote_copy(
                    src_ref=send1.at[h, at],
                    dst_ref=recv1.at[h, o - 1],
                    send_sem=p1_send.at[h, o - 1],
                    recv_sem=p1_recv.at[h, o - 1],
                    device_id={"rep": rep, "tp": dest},
                    device_id_type=MESH,
                )
            )
        return made

    def second_copies(h):
        size = one_axis(h, 1, 0)[0]
        made = []
        for o in range(1, size):
            _, at, dest = one_axis(h, 1, o)
            made.append(
                pltpu.make_async_remote_copy(
                    src_ref=send2.at[h, at],
                    dst_ref=recv2.at[h, o - 1],
                    send_sem=p2_send.at[h, o - 1],
                    recv_sem=p2_recv.at[h, o - 1],
                    device_id={"rep": rep, "tp": dest},
                    device_id_type=MESH,
                )
            )
        return made

    for h in range(2):
        ids = (iota((per * grp, slots), 0) + (h * per * grp + 1)).astype(F32)
        onehot = jnp.where(ids == target_row, 1.0, 0.0).astype(BF)
        for k in range(0, ks, 2):
            placed = jnp.dot(
                onehot, dd[:, k * BLK : (k + 2) * BLK], preferred_element_type=F32
            ).astype(BF)
            for c in range(per):
                for i in range(2):
                    dense[(k + i) * grp : (k + i + 1) * grp, c * BLK : (c + 1) * BLK] = placed[
                        c * grp : (c + 1) * grp, i * BLK : (i + 1) * BLK
                    ]
        wide = 256
        for n in range(cw // wide):
            cols = slice(h * cw + n * wide, h * cw + (n + 1) * wide)
            there = slice(n * wide, (n + 1) * wide)
            total = acc[:, cols] + jnp.dot(hsm[...], dense[:, there], preferred_element_type=F32)
            acc[:, cols] = total
            part = total.astype(BF).reshape(ny, nx, own_rows, wide)
            for yy in range(ny):
                if h == 0:
                    for xx in range(nx):
                        send1[h, xx, yy, :, there] = part[yy, xx]
                else:
                    send1[h, yy, :, :, there] = part[yy]
        for copy in first_copies(h):
            copy.start()

    @pl.when(jnp.logical_not(early))
    def _():
        attend_cached()

    for h in range(2):
        copies = first_copies(h)
        for copy in copies:
            copy.wait_recv()
        cols = slice(h * cw, (h + 1) * cw)
        for a in range(ny if h == 0 else nx):
            row = (a * nx + x if h == 0 else y * nx + a) * own_rows
            total = acc[pl.ds(pl.multiple_of(row, own_rows), own_rows), cols]
            for n in range(len(copies)):
                total = total + recv1[h, n, a].astype(F32)
            mid[h, a] = total
            send2[h, a] = total.astype(BF)
        for copy in second_copies(h):
            copy.start()
    def finish(h):
        copies = second_copies(h)
        for copy in copies:
            copy.wait_recv()
        total = mid[h, y if h == 0 else x]
        for n in range(len(copies)):
            total = total + recv2[h, n].astype(F32)
        new_ref[:, h * cw : (h + 1) * cw] = total.astype(BF)

    finish(0)
    for k in range(KVH):
        own_key = new_ref[:, k * HD : (k + 1) * HD].astype(F32)
        own = (
            jnp.sum(
                head_queries(k).astype(F32) * jnp.concatenate([own_key] * GROUP, axis=0),
                axis=1,
                keepdims=True,
            )
            * scale
        )
        top = mstat[k]
        new_top = jnp.maximum(top, own)
        a = jnp.exp(top - new_top)
        b = jnp.exp(own - new_top)
        inv = 1.0 / (lstat[k] * a + b)
        mixed[k] = mixed[k] * (a * inv)
        lstat[k] = b * inv
    finish(1)
    for k in range(KVH):
        own_value = new_ref[:, (KVH + k) * HD : (KVH + k + 1) * HD].astype(F32)
        out = mixed[k] + lstat[k] * jnp.concatenate([own_value] * GROUP, axis=0)
        out = out.astype(BF)
        for g in range(GROUP):
            at = (k * GROUP + g) * HD
            att_ref[:, at : at + HD] = out[g * own_rows : (g + 1) * own_rows]

    for j in strides:
        for copy in far_copies(j, True):
            copy.wait_send()
    for i, d in enumerate(steps):
        near_copy(i, d, True).wait_send()
    core_copy(True).wait_send()
    hs_wait().wait_send()
    for h in range(2):
        for copy in first_copies(h) + second_copies(h):
            copy.wait_send()


def solution(mesh):
    n_rep, n_tp = mesh.shape["rep"], mesh.shape["tp"]
    nx = 4 if n_tp == 16 else 2
    nz = n_rep // 2
    zlo_n = 8 if nz == 32 else 2
    zhi_n = nz // zlo_n

    def body(hidden, projection, block_index, block_counts, block_change, queries, cached, lengths):
        rows, depth = hidden.shape
        kvw = projection.shape[1]
        own_rows, span = cached.shape[0], cached.shape[1]
        ks = BLK // n_tp
        slots = n_rep * SLOTS
        share = depth // n_tp
        cw = kvw // 2
        heads = GROUP * own_rows
        n2 = zlo_n - 1
        side = nx
        any_spec = pl.BlockSpec(memory_space=pl.ANY)
        smem = pl.BlockSpec(memory_space=pltpu.SMEM)
        vmem = pl.BlockSpec(memory_space=pltpu.VMEM)
        dma = pltpu.SemaphoreType.DMA
        return pl.pallas_call(
            functools.partial(kernel, n_rep, n_tp, nx, zlo_n),
            out_shape=(
                jax.ShapeDtypeStruct((own_rows, kvw), BF),
                jax.ShapeDtypeStruct((own_rows, queries.shape[1]), BF),
            ),
            in_specs=[any_spec, any_spec, smem, smem, any_spec, any_spec, any_spec, smem],
            out_specs=(vmem, vmem),
            scratch_shapes=[
                pltpu.VMEM((rows, depth), BF),
                pltpu.VMEM((depth, kvw), BF),
                pltpu.VMEM(block_change.shape, BF),
                pltpu.VMEM(queries.shape, BF),
                pltpu.VMEM(cached.shape, BF),
                pltpu.VMEM((2, zlo_n, zhi_n + 1, SLOTS * ks, BLK), BF),
                pltpu.VMEM((zhi_n, 1, 128), F32),
                pltpu.VMEM((depth, depth), BF),
                pltpu.VMEM((n_tp, share, rows), BF),
                pltpu.VMEM((n_tp, share, rows), BF),
                pltpu.VMEM((rows, depth), BF),
                pltpu.VMEM((slots * ks, BLK), F32),
                pltpu.VMEM((slots, ks * BLK), BF),
                pltpu.VMEM((depth, cw), BF),
                pltpu.VMEM((rows, kvw), F32),
                pltpu.VMEM((2, side, side, own_rows, cw), BF),
                pltpu.VMEM((2, side - 1, side, own_rows, cw), BF),
                pltpu.VMEM((2, side, own_rows, cw), F32),
                pltpu.VMEM((2, side, own_rows, cw), BF),
                pltpu.VMEM((2, side - 1, own_rows, cw), BF),
                pltpu.VMEM((heads, own_rows * span), F32),
                pltpu.VMEM((KVH, heads, HD), F32),
                pltpu.VMEM((KVH, heads, HD), F32),
                pltpu.VMEM((KVH, heads, HD), F32),
                dma((5,)),
                dma((2, zhi_n - 1)),
                dma((2, zhi_n - 1)),
                dma((n2,)),
                dma((n2,)),
                dma,
                dma,
                dma,
                dma,
                dma((2, side - 1)),
                dma((2, side - 1)),
                dma((2, side - 1)),
                dma((2, side - 1)),
            ],
            compiler_params=pltpu.CompilerParams(
                collective_id=0, has_side_effects=True, vmem_limit_bytes=60 * 1024 * 1024
            ),
        )(hidden, projection, block_index, block_counts, block_change, queries, cached, lengths)

    return jax.shard_map(
        body,
        mesh=mesh,
        in_specs=(
            P("rep", "tp"),
            P("tp", None),
            P("rep", None),
            P("rep"),
            P("rep", None, None, None),
            P(("rep", "tp"), None),
            P(("rep", "tp"), None, None),
            P(("rep", "tp")),
        ),
        out_specs=(P(("rep", "tp"), None), P(("rep", "tp"), None)),
        check_vma=False,
    )
```

```python
import functools
import math

import jax
import jax.numpy as jnp
from jax import lax
from jax.experimental import pallas as pl
from jax.experimental.pallas import tpu as pltpu
from jax.sharding import PartitionSpec as P

QH = 64
KVH = 8
HD = 128
BLK = 128
SLOTS = 2
GROUP = 8
MESH = pl.DeviceIdType.MESH
BF = jnp.bfloat16
F32 = jnp.float32
NEG = -1e30
NT = (((1,), (1,)), ((), ()))
TN = (((0,), (0,)), ((), ()))


def iota(shape, dim):
    return lax.broadcasted_iota(jnp.int32, shape, dim)


def kernel(
    n_rep,
    n_tp,
    nx,
    zlo_n,
    hid_hbm,
    proj_hbm,
    idx_ref,
    cnt_ref,
    chg_hbm,
    q_hbm,
    cache_hbm,
    len_ref,
    new_ref,
    att_ref,
    hid,
    proj,
    chg,
    qs,
    cache,
    gath,
    aim,
    perm,
    hp,
    hs,
    hsm,
    d32,
    dd,
    dense,
    acc,
    send1,
    recv1,
    mid,
    send2,
    recv2,
    bias,
    mixed,
    mstat,
    lstat,
    local_sem,
    s1_send,
    s1_recv,
    s2_send,
    s2_recv,
    s3_send,
    s3_recv,
    hs_send,
    hs_recv,
    p1_send,
    p1_recv,
    p2_send,
    p2_recv,
):
    rep = lax.axis_index("rep")
    tp = lax.axis_index("tp")
    core = rep % 2
    z = rep // 2
    nz = n_rep // 2
    zhi_n = nz // zlo_n
    zlo = z % zlo_n
    zhi = z // zlo_n
    ny = n_tp // nx
    y = tp // nx
    x = tp % nx
    ks = BLK // n_tp
    depth = hid.shape[1]
    rows = hid.shape[0]
    nrb = depth // BLK
    kvw = proj.shape[1]
    own_rows = rows // n_tp
    slots = n_rep * SLOTS
    share = nrb * ks
    parts = 2
    cw = kvw // (2 * parts)
    ncb = kvw // BLK
    tile_rows = SLOTS * ks

    loads = []
    for n, (src, dst) in enumerate(
        ((chg_hbm, chg), (hid_hbm, hid), (proj_hbm, proj), (q_hbm, qs), (cache_hbm, cache))
    ):
        copy = pltpu.make_async_copy(src, dst, local_sem.at[n])
        copy.start()
        loads.append(copy)

    sign = 1 - 2 * core

    def at_z(zz, cc):
        return {"rep": ((zz + 2 * nz) % nz) * 2 + cc, "tp": tp}

    def at_plane(o, direction):
        oy, ox = o // nx, o % nx
        return ((y + direction * oy + ny) % ny) * nx + (x + direction * ox + nx) % nx

    strides = sorted(range(1, zhi_n), key=lambda j: -min(j, zhi_n - j))
    steps = [d for d in range(-(zlo_n // 2 - 1), zlo_n // 2 + 1) if d != 0]
    steps.sort(key=lambda d: -abs(d))

    barrier = pltpu.get_barrier_semaphore()
    for j in strides:
        pl.semaphore_signal(barrier, inc=1, device_id=at_z(z + zlo_n * j, core), device_id_type=MESH)
    for d in steps:
        pl.semaphore_signal(barrier, inc=1, device_id=at_z(z - sign * d, core), device_id_type=MESH)
    pl.semaphore_signal(barrier, inc=1, device_id=at_z(z, 1 - core), device_id_type=MESH)
    for o in range(1, n_tp):
        pl.semaphore_signal(
            barrier, inc=1, device_id={"rep": rep, "tp": at_plane(o, -1)}, device_id_type=MESH
        )

    place = (core * zlo_n + zlo) * zhi_n + zhi
    lane = iota((1, 128), 1)
    row_value = jnp.zeros((1, 128), F32)
    for s in range(SLOTS):
        b = idx_ref[0, s]
        target = (b & (ncb - 1)) * (n_tp * nrb) + (b >> 4) + 1
        target = jnp.where(s < cnt_ref[0], target, 0)
        row_value = jnp.where(lane == place * SLOTS + s, target.astype(F32), row_value)
    aim[zhi] = row_value

    pj = iota((tile_rows, 1), 0)
    pk = iota((1, SLOTS * BLK), 1)
    pick = jnp.where(pk == (pj // ks) * BLK + tp * ks + pj % ks, 1.0, 0.0).astype(BF)
    loads[0].wait()
    own_share = jnp.dot(pick, chg[...].reshape(SLOTS * BLK, BLK), preferred_element_type=F32)
    gath[core, zlo, zhi] = own_share.astype(BF)

    scale = 1.0 / math.sqrt(HD)

    def head_queries(k):
        heads = qs[:, pl.ds(pl.multiple_of(k * GROUP * HD, GROUP * HD), GROUP * HD)]
        return jnp.concatenate([heads[:, g * HD : (g + 1) * HD] for g in range(GROUP)], axis=0)

    def hs_wait():
        return pltpu.make_async_remote_copy(
            src_ref=hs.at[pl.ds(1, n_tp - 1)],
            dst_ref=hs.at[pl.ds(1, n_tp - 1)],
            send_sem=hs_send,
            recv_sem=hs_recv,
            device_id={"rep": rep, "tp": at_plane(1, 1)},
            device_id_type=MESH,
        )

    def project():
        loads[2].wait()
        tile = 512

        @pl.loop(0, kvw // tile)
        def _(n):
            cols = pl.ds(pl.multiple_of(n * tile, tile), tile)
            acc[:, cols] = jnp.dot(hid[...], proj[:, cols], preferred_element_type=F32)

    def attend_cached():
        loads[3].wait()
        loads[4].wait()
        span = cache.shape[1]
        positions = own_rows * span
        pos_lane = iota((1, positions), 1)
        valid_len = jnp.zeros((1, positions), jnp.int32)
        for i in range(own_rows):
            valid_len = jnp.where(pos_lane // span == i, len_ref[i], valid_len)
        seen = jnp.where(pos_lane % span < valid_len, 0.0, NEG)
        same = (
            iota((GROUP * own_rows, positions), 0) % own_rows
            == iota((GROUP * own_rows, positions), 1) // span
        )
        bias[...] = jnp.where(same, seen, NEG)

        @pl.loop(0, KVH)
        def _(k):
            keys = cache[:, :, pl.ds(pl.multiple_of(k * HD, HD), HD)].reshape(positions, HD)
            values = cache[:, :, pl.ds(pl.multiple_of((KVH + k) * HD, HD), HD)].reshape(positions, HD)
            score = lax.dot_general(head_queries(k), keys, NT, preferred_element_type=F32)
            score = score * scale + bias[...]
            top = jnp.max(score, axis=1, keepdims=True)
            e = jnp.exp(score - top)
            hi = e.astype(BF)
            lo = (e - hi.astype(F32)).astype(BF)
            mixed[k] = jnp.dot(hi, values, preferred_element_type=F32) + jnp.dot(
                lo, values, preferred_element_type=F32
            )
            mstat[k] = jnp.broadcast_to(top, (GROUP * own_rows, HD))
            lstat[k] = jnp.broadcast_to(jnp.sum(e, axis=1, keepdims=True), (GROUP * own_rows, HD))

    early = z < (3 * nz) // 8

    loads[1].wait()

    @pl.when(early)
    def _():
        project()
        attend_cached()

    pl.semaphore_wait(barrier, len(strides) + len(steps) + 1 + n_tp - 1)

    def far_copies(j, send):
        zz = zhi if send else (zhi - j + zhi_n) % zhi_n
        return [
            pltpu.make_async_remote_copy(
                src_ref=ref,
                dst_ref=ref,
                send_sem=s1_send.at[m, j - 1],
                recv_sem=s1_recv.at[m, j - 1],
                device_id=at_z(z + zlo_n * j, core),
                device_id_type=MESH,
            )
            for m, ref in enumerate((gath.at[core, zlo, zz], aim.at[zz]))
        ]

    def near_copy(i, d, send):
        zz = zlo if send else (zlo - sign * d + zlo_n) % zlo_n
        return pltpu.make_async_remote_copy(
            src_ref=gath.at[core, zz],
            dst_ref=gath.at[core, zz],
            send_sem=s2_send.at[i],
            recv_sem=s2_recv.at[i],
            device_id=at_z(z + sign * d, core),
            device_id_type=MESH,
        )

    def core_copy(zz, send):
        cc = core if send else 1 - core
        return pltpu.make_async_remote_copy(
            src_ref=gath.at[cc, zz],
            dst_ref=gath.at[cc, zz],
            send_sem=s3_send.at[zz],
            recv_sem=s3_recv.at[zz],
            device_id=at_z(z, 1 - core),
            device_id_type=MESH,
        )

    for j in strides:
        for copy in far_copies(j, True):
            copy.start()

    pj = iota((depth, 1), 0)
    pk = iota((1, depth), 1)
    p1 = ((pj & (share - 1)) // ks) * BLK + (pj // share) * ks + (pj & (ks - 1))
    perm[...] = jnp.where(p1 == pk, 1.0, 0.0).astype(BF)
    hp[...] = (
        lax.dot_general(perm[...], hid[...], NT, preferred_element_type=F32)
        .astype(BF)
        .reshape(hp.shape)
    )
    hs[0] = hp[tp]
    for o in range(1, n_tp):
        dest = at_plane(o, 1)
        pltpu.make_async_remote_copy(
            src_ref=hp.at[dest],
            dst_ref=hs.at[o],
            send_sem=hs_send,
            recv_sem=hs_recv,
            device_id={"rep": rep, "tp": dest},
            device_id_type=MESH,
        ).start()

    for j in strides:
        for copy in far_copies(j, False):
            copy.wait_recv()
    aims = jnp.sum(aim[...].reshape(zhi_n, 128), axis=0, keepdims=True)
    upper = jnp.floor(aims * (1.0 / 32.0))
    line = iota((tile_rows, 128), 0)
    gath[core, zlo, zhi_n] = jnp.where(
        line == 0, upper, jnp.where(line == 1, aims - 32.0 * upper, 0.0)
    ).astype(BF)
    for i, d in enumerate(steps):
        near_copy(i, d, True).start()
    core_copy(zlo, True).start()

    @pl.when(jnp.logical_not(early))
    def _():
        project()

    pj = iota((depth, 1), 0)
    pk = iota((1, depth), 1)
    po = pj // share
    pc = ((y - po // nx + ny) & (ny - 1)) * nx + ((x - (po & (nx - 1)) + nx) & (nx - 1))
    p2 = (pj & (ks - 1)) * (n_tp * nrb) + pc * nrb + (pj & (share - 1)) // ks
    perm[...] = jnp.where(p2 == pk, 1.0, 0.0).astype(BF)

    for i, d in reversed(list(enumerate(steps))):
        near_copy(i, d, False).wait_recv()
        core_copy((zlo - sign * d + zlo_n) % zlo_n, True).start()
    hs_wait().wait_recv()
    hsm[...] = lax.dot_general(
        hs[...].reshape(depth, rows), perm[...], TN, preferred_element_type=F32
    ).astype(BF)

    for zz in range(zlo_n):
        core_copy(zz, False).wait_recv()

    code = jnp.sum(gath[:, :, zhi_n].reshape(2 * zlo_n, tile_rows, 128).astype(F32), axis=0)
    target_row = (code[0:1] * 32.0 + code[1:2])[:, :slots]
    d32[...] = gath[:, :, :zhi_n].reshape(slots * ks, BLK).astype(F32)
    for k in range(ks):
        dd[:, k * BLK : (k + 1) * BLK] = d32[pl.ds(k, slots, stride=ks), :].astype(BF)

    per = cw // BLK
    grp = n_tp * nrb

    def one_axis(h, phase, o):
        along_x = (h + phase) % 2 == 0
        at = ((x if along_x else y) + o) % (nx if along_x else ny)
        return at, (y * nx + at if along_x else at * nx + x)

    def copies(h, c, phase):
        src, dst, sent, got = (
            (send1, recv1, p1_send, p1_recv) if phase == 0 else (send2, recv2, p2_send, p2_recv)
        )
        made = []
        for o in sorted(range(1, nx), key=lambda o: -min(o, nx - o)):
            at, dest = one_axis(h, phase, o)
            made.append(
                pltpu.make_async_remote_copy(
                    src_ref=src.at[h * parts + c, at],
                    dst_ref=dst.at[h * parts + c, o - 1],
                    send_sem=sent.at[h * parts + c, o - 1],
                    recv_sem=got.at[h * parts + c, o - 1],
                    device_id={"rep": rep, "tp": dest},
                    device_id_type=MESH,
                )
            )
        return made

    wide = 256
    chunks = [(h, c) for c in range(parts) for h in range(2)]
    for h, c in chunks:
        hc = h * parts + c
        ids = (iota((per * grp, slots), 0) + (hc * per * grp + 1)).astype(F32)
        onehot = jnp.where(ids == target_row, 1.0, 0.0).astype(BF)
        for k in range(0, ks, 2):
            placed = jnp.dot(
                onehot, dd[:, k * BLK : (k + 2) * BLK], preferred_element_type=F32
            ).astype(BF)
            for b in range(per):
                for i in range(2):
                    dense[(k + i) * grp : (k + i + 1) * grp, b * BLK : (b + 1) * BLK] = placed[
                        b * grp : (b + 1) * grp, i * BLK : (i + 1) * BLK
                    ]
        for n in range(cw // wide):
            cols = slice(hc * cw + n * wide, hc * cw + (n + 1) * wide)
            there = slice(n * wide, (n + 1) * wide)
            total = acc[:, cols] + jnp.dot(hsm[...], dense[:, there], preferred_element_type=F32)
            acc[:, cols] = total
            part = total.astype(BF).reshape(ny, nx, own_rows, wide)
            for yy in range(ny):
                if h == 0:
                    for xx in range(nx):
                        send1[hc, xx, yy, :, there] = part[yy, xx]
                else:
                    send1[hc, yy, :, :, there] = part[yy]
        for copy in copies(h, c, 0):
            copy.start()

    @pl.when(jnp.logical_not(early))
    def _():
        attend_cached()

    for h, c in chunks:
        hc = h * parts + c
        for copy in copies(h, c, 0):
            copy.wait_recv()
        cols = slice(hc * cw, (hc + 1) * cw)
        for a in range(nx):
            row = (a * nx + x if h == 0 else y * nx + a) * own_rows
            total = acc[pl.ds(pl.multiple_of(row, own_rows), own_rows), cols]
            for n in range(nx - 1):
                total = total + recv1[hc, n, a].astype(F32)
            mid[hc, a] = total
            send2[hc, a] = total.astype(BF)
        for copy in copies(h, c, 1):
            copy.start()

    def finish(h):
        for c in range(parts):
            hc = h * parts + c
            for copy in copies(h, c, 1):
                copy.wait_recv()
            total = mid[hc, y if h == 0 else x]
            for n in range(nx - 1):
                total = total + recv2[hc, n].astype(F32)
            new_ref[:, hc * cw : (hc + 1) * cw] = total.astype(BF)

    finish(0)
    for k in range(KVH):
        own_key = new_ref[:, k * HD : (k + 1) * HD].astype(F32)
        own = (
            jnp.sum(
                head_queries(k).astype(F32) * jnp.concatenate([own_key] * GROUP, axis=0),
                axis=1,
                keepdims=True,
            )
            * scale
        )
        top = mstat[k]
        new_top = jnp.maximum(top, own)
        a = jnp.exp(top - new_top)
        b = jnp.exp(own - new_top)
        inv = 1.0 / (lstat[k] * a + b)
        mixed[k] = mixed[k] * (a * inv)
        lstat[k] = b * inv
    finish(1)
    for k in range(KVH):
        own_value = new_ref[:, (KVH + k) * HD : (KVH + k + 1) * HD].astype(F32)
        out = mixed[k] + lstat[k] * jnp.concatenate([own_value] * GROUP, axis=0)
        out = out.astype(BF)
        for g in range(GROUP):
            at = (k * GROUP + g) * HD
            att_ref[:, at : at + HD] = out[g * own_rows : (g + 1) * own_rows]

    for j in strides:
        for copy in far_copies(j, True):
            copy.wait_send()
    for i, d in enumerate(steps):
        near_copy(i, d, True).wait_send()
    for zz in range(zlo_n):
        core_copy(zz, True).wait_send()
    hs_wait().wait_send()
    for h, c in chunks:
        for copy in copies(h, c, 0) + copies(h, c, 1):
            copy.wait_send()


def solution(mesh):
    n_rep, n_tp = mesh.shape["rep"], mesh.shape["tp"]
    nx = 4 if n_tp == 16 else 2
    nz = n_rep // 2
    zlo_n = 8 if nz == 32 else 2
    zhi_n = nz // zlo_n

    def body(hidden, projection, block_index, block_counts, block_change, queries, cached, lengths):
        rows, depth = hidden.shape
        kvw = projection.shape[1]
        own_rows, span = cached.shape[0], cached.shape[1]
        ks = BLK // n_tp
        slots = n_rep * SLOTS
        share = depth // n_tp
        parts = 4
        cw = kvw // parts
        heads = GROUP * own_rows
        n2 = zlo_n - 1
        side = nx
        any_spec = pl.BlockSpec(memory_space=pl.ANY)
        smem = pl.BlockSpec(memory_space=pltpu.SMEM)
        vmem = pl.BlockSpec(memory_space=pltpu.VMEM)
        dma = pltpu.SemaphoreType.DMA
        return pl.pallas_call(
            functools.partial(kernel, n_rep, n_tp, nx, zlo_n),
            out_shape=(
                jax.ShapeDtypeStruct((own_rows, kvw), BF),
                jax.ShapeDtypeStruct((own_rows, queries.shape[1]), BF),
            ),
            in_specs=[any_spec, any_spec, smem, smem, any_spec, any_spec, any_spec, smem],
            out_specs=(vmem, vmem),
            scratch_shapes=[
                pltpu.VMEM((rows, depth), BF),
                pltpu.VMEM((depth, kvw), BF),
                pltpu.VMEM(block_change.shape, BF),
                pltpu.VMEM(queries.shape, BF),
                pltpu.VMEM(cached.shape, BF),
                pltpu.VMEM((2, zlo_n, zhi_n + 1, SLOTS * ks, BLK), BF),
                pltpu.VMEM((zhi_n, 1, 128), F32),
                pltpu.VMEM((depth, depth), BF),
                pltpu.VMEM((n_tp, share, rows), BF),
                pltpu.VMEM((n_tp, share, rows), BF),
                pltpu.VMEM((rows, depth), BF),
                pltpu.VMEM((slots * ks, BLK), F32),
                pltpu.VMEM((slots, ks * BLK), BF),
                pltpu.VMEM((depth, cw), BF),
                pltpu.VMEM((rows, kvw), F32),
                pltpu.VMEM((parts, side, side, own_rows, cw), BF),
                pltpu.VMEM((parts, side - 1, side, own_rows, cw), BF),
                pltpu.VMEM((parts, side, own_rows, cw), F32),
                pltpu.VMEM((parts, side, own_rows, cw), BF),
                pltpu.VMEM((parts, side - 1, own_rows, cw), BF),
                pltpu.VMEM((heads, own_rows * span), F32),
                pltpu.VMEM((KVH, heads, HD), F32),
                pltpu.VMEM((KVH, heads, HD), F32),
                pltpu.VMEM((KVH, heads, HD), F32),
                dma((5,)),
                dma((2, zhi_n - 1)),
                dma((2, zhi_n - 1)),
                dma((n2,)),
                dma((n2,)),
                dma((zlo_n,)),
                dma((zlo_n,)),
                dma,
                dma,
                dma((parts, side - 1)),
                dma((parts, side - 1)),
                dma((parts, side - 1)),
                dma((parts, side - 1)),
            ],
            compiler_params=pltpu.CompilerParams(
                collective_id=0, has_side_effects=True, vmem_limit_bytes=60 * 1024 * 1024
            ),
        )(hidden, projection, block_index, block_counts, block_change, queries, cached, lengths)

    return jax.shard_map(
        body,
        mesh=mesh,
        in_specs=(
            P("rep", "tp"),
            P("tp", None),
            P("rep", None),
            P("rep"),
            P("rep", None, None, None),
            P(("rep", "tp"), None),
            P(("rep", "tp"), None, None),
            P(("rep", "tp")),
        ),
        out_specs=(P(("rep", "tp"), None), P(("rep", "tp"), None)),
        check_vma=False,
    )
```

```python
import functools
import math

import jax
import jax.numpy as jnp
from jax import lax
from jax.experimental import pallas as pl
from jax.experimental.pallas import tpu as pltpu
from jax.sharding import PartitionSpec as P

QH = 64
KVH = 8
HD = 128
BLK = 128
SLOTS = 2
GROUP = 8
MESH = pl.DeviceIdType.MESH
BF = jnp.bfloat16
F32 = jnp.float32
NEG = -1e30
NT = (((1,), (1,)), ((), ()))
TN = (((0,), (0,)), ((), ()))


def iota(shape, dim):
    return lax.broadcasted_iota(jnp.int32, shape, dim)


def kernel(
    n_rep,
    n_tp,
    nx,
    zlo_n,
    hid_hbm,
    proj_hbm,
    idx_ref,
    cnt_ref,
    chg_hbm,
    q_hbm,
    cache_hbm,
    len_ref,
    new_ref,
    att_ref,
    hid,
    proj,
    chg,
    qs,
    cache,
    gath,
    aim,
    perm,
    hp,
    hs,
    hsm,
    d32,
    dd,
    dense,
    acc,
    send1,
    recv1,
    mid,
    send2,
    recv2,
    bias,
    mixed,
    mstat,
    lstat,
    local_sem,
    s1_send,
    s1_recv,
    s2_send,
    s2_recv,
    s3_send,
    s3_recv,
    hs_send,
    hs_recv,
    p1_send,
    p1_recv,
    p2_send,
    p2_recv,
):
    rep = lax.axis_index("rep")
    tp = lax.axis_index("tp")
    core = rep % 2
    z = rep // 2
    nz = n_rep // 2
    zhi_n = nz // zlo_n
    zlo = z % zlo_n
    zhi = z // zlo_n
    ny = n_tp // nx
    y = tp // nx
    x = tp % nx
    ks = BLK // n_tp
    depth = hid.shape[1]
    rows = hid.shape[0]
    nrb = depth // BLK
    kvw = proj.shape[1]
    own_rows = rows // n_tp
    slots = n_rep * SLOTS
    share = nrb * ks
    parts = 2
    cw = kvw // (2 * parts)
    ncb = kvw // BLK
    tile_rows = SLOTS * ks

    loads = []
    for n, (src, dst) in enumerate(
        ((chg_hbm, chg), (hid_hbm, hid), (proj_hbm, proj), (q_hbm, qs), (cache_hbm, cache))
    ):
        copy = pltpu.make_async_copy(src, dst, local_sem.at[n])
        copy.start()
        loads.append(copy)

    sign = 1 - 2 * core

    def at_z(zz, cc):
        return {"rep": ((zz + 2 * nz) % nz) * 2 + cc, "tp": tp}

    def at_plane(o, direction):
        oy, ox = o // nx, o % nx
        return ((y + direction * oy + ny) % ny) * nx + (x + direction * ox + nx) % nx

    strides = sorted(range(1, zhi_n), key=lambda j: -min(j, zhi_n - j))
    steps = [d for d in range(-(zlo_n // 2 - 1), zlo_n // 2 + 1) if d != 0]
    steps.sort(key=lambda d: -abs(d))

    barrier = pltpu.get_barrier_semaphore()
    for j in strides:
        pl.semaphore_signal(barrier, inc=1, device_id=at_z(z + zlo_n * j, core), device_id_type=MESH)
    for d in steps:
        pl.semaphore_signal(barrier, inc=1, device_id=at_z(z - sign * d, core), device_id_type=MESH)
    pl.semaphore_signal(barrier, inc=1, device_id=at_z(z, 1 - core), device_id_type=MESH)
    for o in range(1, n_tp):
        pl.semaphore_signal(
            barrier, inc=1, device_id={"rep": rep, "tp": at_plane(o, -1)}, device_id_type=MESH
        )

    place = (core * zlo_n + zlo) * zhi_n + zhi
    lane = iota((1, 128), 1)
    row_value = jnp.zeros((1, 128), F32)
    for s in range(SLOTS):
        b = idx_ref[0, s]
        target = (b & (ncb - 1)) * (n_tp * nrb) + (b >> 4) + 1
        target = jnp.where(s < cnt_ref[0], target, 0)
        row_value = jnp.where(lane == place * SLOTS + s, target.astype(F32), row_value)
    aim[zhi] = row_value

    pj = iota((tile_rows, 1), 0)
    pk = iota((1, SLOTS * BLK), 1)
    pick = jnp.where(pk == (pj // ks) * BLK + tp * ks + pj % ks, 1.0, 0.0).astype(BF)
    loads[0].wait()
    own_share = jnp.dot(pick, chg[...].reshape(SLOTS * BLK, BLK), preferred_element_type=F32)
    gath[core, zlo, zhi] = own_share.astype(BF)

    scale = 1.0 / math.sqrt(HD)

    def head_queries(k):
        heads = qs[:, pl.ds(pl.multiple_of(k * GROUP * HD, GROUP * HD), GROUP * HD)]
        return jnp.concatenate([heads[:, g * HD : (g + 1) * HD] for g in range(GROUP)], axis=0)

    def hs_wait():
        return pltpu.make_async_remote_copy(
            src_ref=hs.at[pl.ds(1, n_tp - 1)],
            dst_ref=hs.at[pl.ds(1, n_tp - 1)],
            send_sem=hs_send,
            recv_sem=hs_recv,
            device_id={"rep": rep, "tp": at_plane(1, 1)},
            device_id_type=MESH,
        )

    def project():
        loads[2].wait()
        tile = 512

        @pl.loop(0, kvw // tile)
        def _(n):
            cols = pl.ds(pl.multiple_of(n * tile, tile), tile)
            acc[:, cols] = jnp.dot(hid[...], proj[:, cols], preferred_element_type=F32)

    def attend_cached():
        loads[3].wait()
        loads[4].wait()
        span = cache.shape[1]
        positions = own_rows * span
        pos_lane = iota((1, positions), 1)
        valid_len = jnp.zeros((1, positions), jnp.int32)
        for i in range(own_rows):
            valid_len = jnp.where(pos_lane // span == i, len_ref[i], valid_len)
        seen = jnp.where(pos_lane % span < valid_len, 0.0, NEG)
        same = (
            iota((GROUP * own_rows, positions), 0) % own_rows
            == iota((GROUP * own_rows, positions), 1) // span
        )
        bias[...] = jnp.where(same, seen, NEG)

        @pl.loop(0, KVH)
        def _(k):
            keys = cache[:, :, pl.ds(pl.multiple_of(k * HD, HD), HD)].reshape(positions, HD)
            values = cache[:, :, pl.ds(pl.multiple_of((KVH + k) * HD, HD), HD)].reshape(positions, HD)
            score = lax.dot_general(head_queries(k), keys, NT, preferred_element_type=F32)
            score = score * scale + bias[...]
            top = jnp.max(score, axis=1, keepdims=True)
            e = jnp.exp(score - top)
            hi = e.astype(BF)
            lo = (e - hi.astype(F32)).astype(BF)
            mixed[k] = jnp.dot(hi, values, preferred_element_type=F32) + jnp.dot(
                lo, values, preferred_element_type=F32
            )
            mstat[k] = jnp.broadcast_to(top, (GROUP * own_rows, HD))
            lstat[k] = jnp.broadcast_to(jnp.sum(e, axis=1, keepdims=True), (GROUP * own_rows, HD))

    early = z < (3 * nz) // 8

    loads[1].wait()

    @pl.when(early)
    def _():
        project()
        attend_cached()

    pl.semaphore_wait(barrier, len(strides) + len(steps) + 1 + n_tp - 1)

    def far_copies(j, send):
        zz = zhi if send else (zhi - j + zhi_n) % zhi_n
        return [
            pltpu.make_async_remote_copy(
                src_ref=ref,
                dst_ref=ref,
                send_sem=s1_send.at[m, j - 1],
                recv_sem=s1_recv.at[m, j - 1],
                device_id=at_z(z + zlo_n * j, core),
                device_id_type=MESH,
            )
            for m, ref in enumerate((gath.at[core, zlo, zz], aim.at[zz]))
        ]

    def near_copy(i, d, send):
        zz = zlo if send else (zlo - sign * d + zlo_n) % zlo_n
        return pltpu.make_async_remote_copy(
            src_ref=gath.at[core, zz],
            dst_ref=gath.at[core, zz],
            send_sem=s2_send.at[i],
            recv_sem=s2_recv.at[i],
            device_id=at_z(z + sign * d, core),
            device_id_type=MESH,
        )

    def core_copy(zz, send):
        cc = core if send else 1 - core
        return pltpu.make_async_remote_copy(
            src_ref=gath.at[cc, zz],
            dst_ref=gath.at[cc, zz],
            send_sem=s3_send.at[zz],
            recv_sem=s3_recv.at[zz],
            device_id=at_z(z, 1 - core),
            device_id_type=MESH,
        )

    for j in strides:
        for copy in far_copies(j, True):
            copy.start()

    pj = iota((depth, 1), 0)
    pk = iota((1, depth), 1)
    p1 = ((pj & (share - 1)) // ks) * BLK + (pj // share) * ks + (pj & (ks - 1))
    perm[...] = jnp.where(p1 == pk, 1.0, 0.0).astype(BF)
    hp[...] = (
        lax.dot_general(perm[...], hid[...], NT, preferred_element_type=F32)
        .astype(BF)
        .reshape(hp.shape)
    )
    hs[0] = hp[tp]
    for o in range(1, n_tp):
        dest = at_plane(o, 1)
        pltpu.make_async_remote_copy(
            src_ref=hp.at[dest],
            dst_ref=hs.at[o],
            send_sem=hs_send,
            recv_sem=hs_recv,
            device_id={"rep": rep, "tp": dest},
            device_id_type=MESH,
        ).start()

    for j in strides:
        for copy in far_copies(j, False):
            copy.wait_recv()
    aims = jnp.sum(aim[...].reshape(zhi_n, 128), axis=0, keepdims=True)
    upper = jnp.floor(aims * (1.0 / 32.0))
    line = iota((tile_rows, 128), 0)
    gath[core, zlo, zhi_n] = jnp.where(
        line == 0, upper, jnp.where(line == 1, aims - 32.0 * upper, 0.0)
    ).astype(BF)
    for i, d in enumerate(steps):
        near_copy(i, d, True).start()
    core_copy(zlo, True).start()

    @pl.when(jnp.logical_not(early))
    def _():
        project()

    pj = iota((depth, 1), 0)
    pk = iota((1, depth), 1)
    po = pj // share
    pc = ((y - po // nx + ny) & (ny - 1)) * nx + ((x - (po & (nx - 1)) + nx) & (nx - 1))
    p2 = (pj & (ks - 1)) * (n_tp * nrb) + pc * nrb + (pj & (share - 1)) // ks
    perm[...] = jnp.where(p2 == pk, 1.0, 0.0).astype(BF)

    for i, d in reversed(list(enumerate(steps))):
        near_copy(i, d, False).wait_recv()
        core_copy((zlo - sign * d + zlo_n) % zlo_n, True).start()
    hs_wait().wait_recv()
    hsm[...] = lax.dot_general(
        hs[...].reshape(depth, rows), perm[...], TN, preferred_element_type=F32
    ).astype(BF)

    for zz in range(zlo_n):
        core_copy(zz, False).wait_recv()

    code = jnp.sum(gath[:, :, zhi_n].reshape(2 * zlo_n, tile_rows, 128).astype(F32), axis=0)
    target_row = (code[0:1] * 32.0 + code[1:2])[:, :slots]
    d32[...] = gath[:, :, :zhi_n].reshape(slots * ks, BLK).astype(F32)
    for k in range(ks):
        dd[:, k * BLK : (k + 1) * BLK] = d32[pl.ds(k, slots, stride=ks), :].astype(BF)

    per = cw // BLK
    grp = n_tp * nrb

    def one_axis(h, phase, o):
        along_x = (h + phase) % 2 == 0
        at = ((x if along_x else y) + o) % (nx if along_x else ny)
        return at, (y * nx + at if along_x else at * nx + x)

    def copies(h, c, phase):
        src, dst, sent, got = (
            (send1, recv1, p1_send, p1_recv) if phase == 0 else (send2, recv2, p2_send, p2_recv)
        )
        made = []
        for o in sorted(range(1, nx), key=lambda o: -min(o, nx - o)):
            at, dest = one_axis(h, phase, o)
            made.append(
                pltpu.make_async_remote_copy(
                    src_ref=src.at[h * parts + c, at],
                    dst_ref=dst.at[h * parts + c, o - 1],
                    send_sem=sent.at[h * parts + c, o - 1],
                    recv_sem=got.at[h * parts + c, o - 1],
                    device_id={"rep": rep, "tp": dest},
                    device_id_type=MESH,
                )
            )
        return made

    wide = 256
    chunks = [(h, c) for c in range(parts) for h in range(2)]
    for h, c in chunks:
        hc = h * parts + c
        ids = (iota((per * grp, slots), 0) + (hc * per * grp + 1)).astype(F32)
        onehot = jnp.where(ids == target_row, 1.0, 0.0).astype(BF)
        for k in range(0, ks, 2):
            placed = jnp.dot(
                onehot, dd[:, k * BLK : (k + 2) * BLK], preferred_element_type=F32
            ).astype(BF)
            for b in range(per):
                for i in range(2):
                    dense[(k + i) * grp : (k + i + 1) * grp, b * BLK : (b + 1) * BLK] = placed[
                        b * grp : (b + 1) * grp, i * BLK : (i + 1) * BLK
                    ]
        for n in range(cw // wide):
            cols = slice(hc * cw + n * wide, hc * cw + (n + 1) * wide)
            there = slice(n * wide, (n + 1) * wide)
            total = acc[:, cols] + jnp.dot(hsm[...], dense[:, there], preferred_element_type=F32)
            acc[:, cols] = total
            part = total.astype(BF).reshape(ny, nx, own_rows, wide)
            for yy in range(ny):
                if h == 0:
                    for xx in range(nx):
                        send1[hc, xx, yy, :, there] = part[yy, xx]
                else:
                    send1[hc, yy, :, :, there] = part[yy]
        for copy in copies(h, c, 0):
            copy.start()

    @pl.when(jnp.logical_not(early))
    def _():
        attend_cached()

    for h, c in chunks:
        hc = h * parts + c
        for copy in copies(h, c, 0):
            copy.wait_recv()
        cols = slice(hc * cw, (hc + 1) * cw)
        for a in range(nx):
            row = (a * nx + x if h == 0 else y * nx + a) * own_rows
            total = acc[pl.ds(pl.multiple_of(row, own_rows), own_rows), cols]
            for n in range(nx - 1):
                total = total + recv1[hc, n, a].astype(F32)
            mid[hc, a] = total
            send2[hc, a] = total.astype(BF)
        for copy in copies(h, c, 1):
            copy.start()

    def finish(h):
        for c in range(parts):
            hc = h * parts + c
            for copy in copies(h, c, 1):
                copy.wait_recv()
            total = mid[hc, y if h == 0 else x]
            for n in range(nx - 1):
                total = total + recv2[hc, n].astype(F32)
            new_ref[:, hc * cw : (hc + 1) * cw] = total.astype(BF)

    finish(0)
    for k in range(KVH):
        own_key = new_ref[:, k * HD : (k + 1) * HD].astype(F32)
        own = (
            jnp.sum(
                head_queries(k).astype(F32) * jnp.concatenate([own_key] * GROUP, axis=0),
                axis=1,
                keepdims=True,
            )
            * scale
        )
        top = mstat[k]
        new_top = jnp.maximum(top, own)
        a = jnp.exp(top - new_top)
        b = jnp.exp(own - new_top)
        inv = 1.0 / (lstat[k] * a + b)
        mixed[k] = mixed[k] * (a * inv)
        lstat[k] = b * inv
    finish(1)
    for k in range(KVH):
        own_value = new_ref[:, (KVH + k) * HD : (KVH + k + 1) * HD].astype(F32)
        out = mixed[k] + lstat[k] * jnp.concatenate([own_value] * GROUP, axis=0)
        out = out.astype(BF)
        for g in range(GROUP):
            at = (k * GROUP + g) * HD
            att_ref[:, at : at + HD] = out[g * own_rows : (g + 1) * own_rows]

    for j in strides:
        for copy in far_copies(j, True):
            copy.wait_send()
    for i, d in enumerate(steps):
        near_copy(i, d, True).wait_send()
    for zz in range(zlo_n):
        core_copy(zz, True).wait_send()
    hs_wait().wait_send()
    for h, c in chunks:
        for copy in copies(h, c, 0) + copies(h, c, 1):
            copy.wait_send()


def solution(mesh):
    n_rep, n_tp = mesh.shape["rep"], mesh.shape["tp"]
    nx = 4 if n_tp == 16 else 2
    nz = n_rep // 2
    zlo_n = 4 if nz == 32 else 2
    zhi_n = nz // zlo_n

    def body(hidden, projection, block_index, block_counts, block_change, queries, cached, lengths):
        rows, depth = hidden.shape
        kvw = projection.shape[1]
        own_rows, span = cached.shape[0], cached.shape[1]
        ks = BLK // n_tp
        slots = n_rep * SLOTS
        share = depth // n_tp
        parts = 4
        cw = kvw // parts
        heads = GROUP * own_rows
        n2 = zlo_n - 1
        side = nx
        any_spec = pl.BlockSpec(memory_space=pl.ANY)
        smem = pl.BlockSpec(memory_space=pltpu.SMEM)
        vmem = pl.BlockSpec(memory_space=pltpu.VMEM)
        dma = pltpu.SemaphoreType.DMA
        return pl.pallas_call(
            functools.partial(kernel, n_rep, n_tp, nx, zlo_n),
            out_shape=(
                jax.ShapeDtypeStruct((own_rows, kvw), BF),
                jax.ShapeDtypeStruct((own_rows, queries.shape[1]), BF),
            ),
            in_specs=[any_spec, any_spec, smem, smem, any_spec, any_spec, any_spec, smem],
            out_specs=(vmem, vmem),
            scratch_shapes=[
                pltpu.VMEM((rows, depth), BF),
                pltpu.VMEM((depth, kvw), BF),
                pltpu.VMEM(block_change.shape, BF),
                pltpu.VMEM(queries.shape, BF),
                pltpu.VMEM(cached.shape, BF),
                pltpu.VMEM((2, zlo_n, zhi_n + 1, SLOTS * ks, BLK), BF),
                pltpu.VMEM((zhi_n, 1, 128), F32),
                pltpu.VMEM((depth, depth), BF),
                pltpu.VMEM((n_tp, share, rows), BF),
                pltpu.VMEM((n_tp, share, rows), BF),
                pltpu.VMEM((rows, depth), BF),
                pltpu.VMEM((slots * ks, BLK), F32),
                pltpu.VMEM((slots, ks * BLK), BF),
                pltpu.VMEM((depth, cw), BF),
                pltpu.VMEM((rows, kvw), F32),
                pltpu.VMEM((parts, side, side, own_rows, cw), BF),
                pltpu.VMEM((parts, side - 1, side, own_rows, cw), BF),
                pltpu.VMEM((parts, side, own_rows, cw), F32),
                pltpu.VMEM((parts, side, own_rows, cw), BF),
                pltpu.VMEM((parts, side - 1, own_rows, cw), BF),
                pltpu.VMEM((heads, own_rows * span), F32),
                pltpu.VMEM((KVH, heads, HD), F32),
                pltpu.VMEM((KVH, heads, HD), F32),
                pltpu.VMEM((KVH, heads, HD), F32),
                dma((5,)),
                dma((2, zhi_n - 1)),
                dma((2, zhi_n - 1)),
                dma((n2,)),
                dma((n2,)),
                dma((zlo_n,)),
                dma((zlo_n,)),
                dma,
                dma,
                dma((parts, side - 1)),
                dma((parts, side - 1)),
                dma((parts, side - 1)),
                dma((parts, side - 1)),
            ],
            compiler_params=pltpu.CompilerParams(
                collective_id=0, has_side_effects=True, vmem_limit_bytes=60 * 1024 * 1024
            ),
        )(hidden, projection, block_index, block_counts, block_change, queries, cached, lengths)

    return jax.shard_map(
        body,
        mesh=mesh,
        in_specs=(
            P("rep", "tp"),
            P("tp", None),
            P("rep", None),
            P("rep"),
            P("rep", None, None, None),
            P(("rep", "tp"), None),
            P(("rep", "tp"), None, None),
            P(("rep", "tp")),
        ),
        out_specs=(P(("rep", "tp"), None), P(("rep", "tp"), None)),
        check_vma=False,
    )
```
